32 devices in a mesh: dp: 4 (over y, x), fsdp: 8 (over z, core).
Axes of the slice: x: 2, y: 2, z: 4, core: 2. Of those that a mesh axis runs over, the one named last changes fastest.
Arguments:
- x_src: bfloat16 [256, 8192], P('fsdp', 'dp'), may hold values from -6 to 6
- doc_lengths: int32 [8, 4], replicated, may hold values from 1 to 16, as said below
- doc_dests: int32 [8, 4], replicated, may hold values from 0 to 7, as said below
- w_gate: bfloat16 [8192, 14336], P('dp', 'fsdp'), may hold values from -0.0625 to 0.0625
- w_up: bfloat16 [8192, 14336], P('dp', 'fsdp'), may hold values from -0.0625 to 0.0625
- w_down: bfloat16 [14336, 8192], P('fsdp', 'dp'), may hold values from -0.046875 to 0.046875
- basis: float32 [8192, 512], P('dp'), may hold values from -0.0625 to 0.0625
- out_cotangent: bfloat16 [512, 8192], P('fsdp', 'dp'), may hold values from -6 to 6
Outputs:
- layer_out: bfloat16 [512, 8192], P('fsdp', 'dp')
- input_grad: bfloat16 [512, 8192], P('fsdp', 'dp')
- grad_gate: float32 [8192, 14336], P('dp', 'fsdp')
- grad_up: float32 [8192, 14336], P('dp', 'fsdp')
- grad_down: float32 [14336, 8192], P('fsdp', 'dp')
The draws below stay inside these ranges and needn't reach their ends.
Inputs may be any that keep to these rules, and one draw needn't show every extreme that they name: `doc_lengths`: the 4 lengths of a source sum to 32 and one of them equals 16. `doc_dests`: document c of every source s goes to destination (s + o_c) modulo 8, for 4 different offsets o_c shared by all sources, one of which is 4; a destination receives at most 64 tokens in all, and some destination receives exactly 64.
All inputs are finite; a program needn't handle non-finite values.
Results may differ from the reference program's by a relative error of at most 0.034.
Values may be sent and summed in bfloat16 or wider, within the bound.
A program may use at most 192 MiB of HBM per device.

```python
import jax
import jax.numpy as jnp
from jax import lax

D = 8192
FW = 14336
KEYS = 512
TOK_SRC = 32
NDOC = 4
MOST = 16
RECV = 64
SOURCES = 8
N_DP = 4
N_FSDP = 8


def deal_plan(key):
    base = jax.random.fold_in(key, 7)
    keys_all = jax.random.split(base, 6)
    half = SOURCES // 2
    others = jax.random.permutation(keys_all[0], SOURCES - 1)[:NDOC - 1].astype(jnp.int32)
    others = others + (others >= half).astype(jnp.int32)
    shifts = jnp.concatenate([jnp.full((1,), half, jnp.int32), others])
    order = jax.random.permutation(keys_all[5], NDOC).astype(jnp.int32)
    shifts = jnp.take(shifts, order).astype(jnp.int32)
    sources = jnp.arange(SOURCES, dtype=jnp.int32)
    dests = (sources[:, None] + shifts[None, :]) % SOURCES
    root = jax.random.randint(keys_all[1], (), 0, SOURCES).astype(jnp.int32)
    longpos = jax.random.randint(keys_all[2], (SOURCES,), 0, NDOC).astype(jnp.int32)
    special = (root - shifts) % SOURCES
    match = (sources[:, None] == special[None, :]).astype(jnp.int32)
    docs = jnp.arange(NDOC, dtype=jnp.int32)
    forced = jnp.sum(match * docs[None, :], axis=1)
    longpos = jnp.where(jnp.sum(match, axis=1) > 0, forced, longpos)
    first_cut = jax.random.randint(keys_all[3], (SOURCES,), 1, MOST).astype(jnp.int32)
    second_cut = jax.random.randint(keys_all[4], (SOURCES,), 1, MOST - 1).astype(jnp.int32)
    second_cut = second_cut + (second_cut >= first_cut).astype(jnp.int32)
    lower = jnp.minimum(first_cut, second_cut)
    upper = jnp.maximum(first_cut, second_cut)
    parts = jnp.stack([lower, upper - lower, MOST - upper], axis=1)
    rank = docs[None, :] - (docs[None, :] > longpos[:, None]).astype(jnp.int32)
    rank = jnp.clip(rank, 0, 2)
    picked = jnp.take_along_axis(parts, rank, axis=1)
    lengths = jnp.where(docs[None, :] == longpos[:, None], MOST, picked)
    return (lengths.astype(jnp.int32), dests.astype(jnp.int32))


def draw_doc_lengths(key, part):
    return deal_plan(key)[0]


def draw_doc_dests(key, part):
    return deal_plan(key)[1]


def steps_of(stream_key, extent, cuts, least, largest):
    level = 1.0
    for position, shards_of in cuts:
        heights = jax.random.uniform(jax.random.fold_in(jax.random.fold_in(stream_key, 6), position), (shards_of,), jnp.float32, least / len(cuts), largest / len(cuts))
        level = level * jnp.repeat(jnp.exp(heights), extent[position] // shards_of).reshape((-1,) + (1,) * (len(extent) - 1 - position))
    return level


def noise(own_key, shape, deviation, bound, shards=(), kind=jnp.bfloat16):
    result = deviation * jax.random.normal(own_key, shape, jnp.float32)
    if shards:
        result = result * steps_of(own_key, shape, shards, -0.22, 0.18)
    return jnp.clip(result, -bound, bound).astype(kind)


def setup_inputs(seed: int = 0) -> dict:
    key_of = jax.random.split(jax.random.key(seed), 9)
    x_src = noise(key_of[0], (SOURCES * TOK_SRC, D), 1.0, 6.0, ((0, 8), (1, 4)))
    doc_lengths = draw_doc_lengths(jax.random.fold_in(key_of[8], 71), 0)
    doc_dests = draw_doc_dests(jax.random.fold_in(key_of[8], 71), 0)
    w_gate = noise(key_of[3], (D, FW), D ** -0.5, 0.0625, ((0, 4), (1, 8)))
    w_up = noise(key_of[4], (D, FW), D ** -0.5, 0.0625, ((0, 4), (1, 8)))
    w_down = noise(key_of[5], (FW, D), FW ** -0.5, 0.046875, ((0, 8), (1, 4)))
    basis = noise(key_of[6], (D, KEYS), D ** -0.5, 0.0625, ((0, 4),), jnp.float32)
    out_cotangent = noise(key_of[7], (SOURCES * RECV, D), 1.0, 6.0, ((0, 8), (1, 4)))
    return dict(x_src=x_src, doc_lengths=doc_lengths, doc_dests=doc_dests, w_gate=w_gate, w_up=w_up, w_down=w_down, basis=basis, out_cotangent=out_cotangent)


def deal_tables(doc_lengths, doc_dests):
    starts = (jnp.cumsum(doc_lengths, axis=1) - doc_lengths).astype(jnp.int32)
    targets = jnp.arange(SOURCES, dtype=jnp.int32)
    hits = (doc_dests[:, :, None] == targets[None, None, :]).astype(jnp.int32)
    loads = jnp.sum(doc_lengths[:, :, None] * hits, axis=1).astype(jnp.int32)
    firsts = jnp.sum(starts[:, :, None] * hits, axis=1).astype(jnp.int32)
    return loads, firsts


def settle(term):
    return lax.optimization_barrier(term.astype(jnp.bfloat16)).astype(jnp.float32)


def split_sum(parts, term, shape):
    def step(k, total):
        return total + settle(term(k))
    return lax.fori_loop(0, parts, step, jnp.zeros(shape, jnp.float32))


def reference(x_src, doc_lengths, doc_dests, w_gate, w_up, w_down, basis, out_cotangent):
    loads, firsts = deal_tables(doc_lengths, doc_dests)
    offsets = (jnp.cumsum(loads, axis=0) - loads).astype(jnp.int32)
    ends = offsets + loads
    place = jnp.arange(RECV, dtype=jnp.int32)
    owner = jnp.sum((ends[:, :, None] <= place[None, None, :]).astype(jnp.int32), axis=0)
    owner = jnp.minimum(owner, SOURCES - 1)
    pick = (owner[None, :, :] == jnp.arange(SOURCES, dtype=jnp.int32)[:, None, None]).astype(jnp.int32)
    own_offset = jnp.sum(pick * offsets[:, :, None], axis=0)
    own_first = jnp.sum(pick * firsts[:, :, None], axis=0)
    valid = place[None, :] < jnp.sum(loads, axis=0)[:, None]
    index = owner * TOK_SRC + own_first + place[None, :] - own_offset
    index = jnp.where(valid, index, 0).astype(jnp.int32).reshape(-1)
    dealt = jnp.take(x_src, index, axis=0)
    dealt = jnp.where(valid.reshape(-1)[:, None], dealt, jnp.zeros_like(dealt))
    rows = dealt.shape[0]
    feat = D // N_DP
    unit = FW // N_FSDP
    contract_cols = (((1,), (1,)), ((), ()))

    def gate_term(k):
        start = (k * feat).astype(jnp.int32)
        block = lax.dynamic_slice_in_dim(dealt, start, feat, 1)
        return jnp.dot(block, lax.dynamic_slice_in_dim(w_gate, start, feat, 0), preferred_element_type=jnp.float32)

    def up_term(k):
        start = (k * feat).astype(jnp.int32)
        block = lax.dynamic_slice_in_dim(dealt, start, feat, 1)
        return jnp.dot(block, lax.dynamic_slice_in_dim(w_up, start, feat, 0), preferred_element_type=jnp.float32)

    gate = split_sum(N_DP, gate_term, (rows, FW))
    up = split_sum(N_DP, up_term, (rows, FW))
    hidden = (jax.nn.silu(gate) * up).astype(jnp.bfloat16)

    def out_term(j):
        start = (j * unit).astype(jnp.int32)
        block = lax.dynamic_slice_in_dim(hidden, start, unit, 1)
        return jnp.dot(block, lax.dynamic_slice_in_dim(w_down, start, unit, 0), preferred_element_type=jnp.float32)

    layer_out = split_sum(N_FSDP, out_term, (rows, D)).astype(jnp.bfloat16)

    def hgrad_term(k):
        start = (k * feat).astype(jnp.int32)
        block = lax.dynamic_slice_in_dim(out_cotangent, start, feat, 1)
        wpart = lax.dynamic_slice_in_dim(w_down, start, feat, 1)
        return lax.dot_general(block, wpart, contract_cols, preferred_element_type=jnp.float32)

    hidden_grad = split_sum(N_DP, hgrad_term, (rows, FW))
    sig = jax.nn.sigmoid(gate)
    gate_grad = (hidden_grad * up * sig * (1.0 + gate * (1.0 - sig))).astype(jnp.bfloat16)
    up_grad = (hidden_grad * gate * sig).astype(jnp.bfloat16)
    grad_down = lax.dot_general(hidden, out_cotangent, (((0,), (0,)), ((), ())), preferred_element_type=jnp.float32)
    raw_gate = lax.dot_general(dealt, gate_grad, (((0,), (0,)), ((), ())), preferred_element_type=jnp.float32)
    raw_up = lax.dot_general(dealt, up_grad, (((0,), (0,)), ((), ())), preferred_element_type=jnp.float32)
    high = lax.Precision.HIGHEST
    over_gate = lax.dot_general(basis, raw_gate, (((0,), (0,)), ((), ())), precision=high)
    grad_gate = raw_gate - jnp.dot(basis, over_gate, precision=high)
    over_up = lax.dot_general(basis, raw_up, (((0,), (0,)), ((), ())), precision=high)
    grad_up = raw_up - jnp.dot(basis, over_up, precision=high)

    def in_term(j):
        start = (j * unit).astype(jnp.int32)
        first = lax.dot_general(lax.dynamic_slice_in_dim(gate_grad, start, unit, 1), lax.dynamic_slice_in_dim(w_gate, start, unit, 1), contract_cols, preferred_element_type=jnp.float32)
        second = lax.dot_general(lax.dynamic_slice_in_dim(up_grad, start, unit, 1), lax.dynamic_slice_in_dim(w_up, start, unit, 1), contract_cols, preferred_element_type=jnp.float32)
        return first + second

    input_grad = split_sum(N_FSDP, in_term, (rows, D)).astype(jnp.bfloat16)
    return layer_out, input_grad, grad_gate, grad_up, grad_down
```

```python
import jax
import jax.numpy as jnp
from jax import lax
from jax.sharding import PartitionSpec as P

DP, FS = "dp", "fsdp"
F32, BF = jnp.float32, jnp.bfloat16
ROWS = (((0,), (0,)), ((), ()))
COLS = (((1,), (1,)), ((), ()))


def dot(a, b, dims=(((1,), (0,)), ((), ())), **kw):
    return lax.dot_general(a, b, dims, preferred_element_type=F32, **kw)


def places(doc_lengths, doc_dests, tokens, recv):
    groups, docs = doc_lengths.shape
    earlier = jnp.arange(docs)[:, None] < jnp.arange(docs)[None, :]
    starts = jnp.sum(doc_lengths[:, :, None] * earlier[None], axis=1)
    same = doc_dests[:, :, None, None] == doc_dests[None, None]
    before = jnp.arange(groups)[:, None] < jnp.arange(groups)[None, :]
    same = same & before[:, None, :, None]
    offsets = jnp.sum(jnp.where(same, doc_lengths[:, :, None, None], 0), axis=(0, 1))
    base = doc_dests * recv + offsets - starts
    t = jnp.arange(tokens)[None, :, None]
    inside = (t >= starts[:, None, :]) & (t < (starts + doc_lengths)[:, None, :])
    place = jnp.sum(jnp.where(inside, base[:, None, :] + t, 0), axis=2)
    return place.reshape(1, groups * tokens).astype(jnp.int32)


def gather(x, axis):
    return lax.all_gather(x, axis, axis=0, tiled=True)


def scatter(x, axis):
    return lax.psum_scatter(x, axis, scatter_dimension=0, tiled=True)


def per_device(x_src, doc_lengths, doc_dests, w_gate, w_up, w_down, basis, dy):
    groups = doc_lengths.shape[0]
    tokens, recv = x_src.shape[0], dy.shape[0]
    width = w_gate.shape[1]
    high = lax.Precision.HIGH
    place = places(doc_lengths, doc_dests, tokens, recv)
    deal = (lax.broadcasted_iota(jnp.int32, (groups * recv, groups * tokens), 0) == place).astype(BF)

    x = gather(x_src, FS)
    g = dot(x, w_gate).astype(BF)
    u = dot(x, w_up).astype(BF)
    q = dot(x.astype(F32), basis, precision=high).astype(BF)
    both = scatter(jnp.concatenate([g, u, q], axis=1), DP).astype(F32)
    gate, up, keys = both[:, :width], both[:, width : 2 * width], both[:, 2 * width :]
    sig = jax.nn.sigmoid(gate)
    hidden = (gate * sig * up).astype(BF)

    dy_all = dot(deal, gather(dy, FS), ROWS).astype(BF)
    hg = scatter(dot(dy_all, w_down, COLS).astype(BF), DP).astype(F32)
    gate_grad = (hg * up * sig * (1.0 + gate * (1.0 - sig))).astype(BF)
    up_grad = (hg * gate * sig).astype(BF)

    first = gather(jnp.concatenate([hidden, keys.astype(BF)], axis=1), DP)
    hall, kall = first[:, :width], first[:, width:]
    second = gather(jnp.concatenate([gate_grad, up_grad], axis=1), DP)
    ggall, ugall = second[:, :width], second[:, width:]

    part = dot(hall, w_down).astype(BF)
    layer_out = scatter(dot(deal, part).astype(BF), FS)
    part = (dot(ggall, w_gate, COLS) + dot(ugall, w_up, COLS)).astype(BF)
    input_grad = scatter(dot(deal, part).astype(BF), FS)

    x_proj = (x.astype(F32) - dot(kall.astype(F32), basis, COLS, precision=high)).astype(BF)
    grad_down = dot(hall, dy_all, ROWS)
    grad_gate = dot(x_proj, ggall, ROWS)
    grad_up = dot(x_proj, ugall, ROWS)
    return layer_out, input_grad, grad_gate, grad_up, grad_down


def solution(mesh):
    tiled = P(FS, DP)
    return jax.shard_map(
        per_device,
        mesh=mesh,
        in_specs=(tiled, P(), P(), P(DP, FS), P(DP, FS), tiled, P(DP, None), tiled),
        out_specs=(tiled, tiled, P(DP, FS), P(DP, FS), tiled),
        check_vma=False,
    )
```

```python
import jax
import jax.numpy as jnp
from jax import lax
from jax.sharding import PartitionSpec as P

DP, FS = "dp", "fsdp"
F32, BF = jnp.float32, jnp.bfloat16
ROWS = (((0,), (0,)), ((), ()))
COLS = (((1,), (1,)), ((), ()))


def dot(a, b, dims=(((1,), (0,)), ((), ())), **kw):
    return lax.dot_general(a, b, dims, preferred_element_type=F32, **kw)


def places(doc_lengths, doc_dests, tokens, recv):
    groups, docs = doc_lengths.shape
    earlier = jnp.arange(docs)[:, None] < jnp.arange(docs)[None, :]
    starts = jnp.sum(doc_lengths[:, :, None] * earlier[None], axis=1)
    same = doc_dests[:, :, None, None] == doc_dests[None, None]
    before = jnp.arange(groups)[:, None] < jnp.arange(groups)[None, :]
    same = same & before[:, None, :, None]
    offsets = jnp.sum(jnp.where(same, doc_lengths[:, :, None, None], 0), axis=(0, 1))
    base = doc_dests * recv + offsets - starts
    t = jnp.arange(tokens)[None, :, None]
    inside = (t >= starts[:, None, :]) & (t < (starts + doc_lengths)[:, None, :])
    place = jnp.sum(jnp.where(inside, base[:, None, :] + t, 0), axis=2)
    return place.reshape(1, groups * tokens).astype(jnp.int32)


def swap(x, axis, k):
    n = lax.axis_size(axis)
    return lax.ppermute(x, axis, [(i, i ^ k) for i in range(n)])


def join(parts, rows, me):
    out = jnp.zeros((len(parts) * rows, parts[0].shape[1]), parts[0].dtype)
    for k, part in enumerate(parts):
        out = lax.dynamic_update_slice(out, part, ((me ^ k) * rows, 0))
    return out


def gather(x, axis, after=None):
    n, me = lax.axis_size(axis), lax.axis_index(axis)
    if axis == DP:
        parts = [x] + [swap(x, axis, k) for k in range(1, n)]
    else:
        same = [x] + [swap(x, axis, k) for k in range(2, n, 2)]
        if after is None:
            parts = [p for s in same for p in (s, swap(s, axis, 1))]
        else:
            mine, _ = lax.optimization_barrier((jnp.concatenate(same, axis=0), after))
            rows, other = x.shape[0], swap(mine, axis, 1)
            cut = lambda a, i: a[i * rows : (i + 1) * rows]
            parts = [p for i in range(n // 2) for p in (cut(mine, i), cut(other, i))]
    return join(parts, x.shape[0], me)


def scatter(x, axis, later=None):
    n, me = lax.axis_size(axis), lax.axis_index(axis)
    rows = x.shape[0] // n
    if axis == DP:
        cut = x.reshape(n, rows, -1)
        pick = lambda i: lax.dynamic_index_in_dim(cut, i, 0, keepdims=False)
        total = pick(me).astype(F32)
        for k in range(1, n):
            total = total + swap(pick(me ^ k), axis, k).astype(F32)
        return total
    pairs = x.reshape(n // 2, 2, rows, -1)
    core = me % 2
    pick = lambda i: lax.dynamic_index_in_dim(pairs, i, 1, keepdims=False)
    both = (pick(core).astype(F32) + swap(pick(1 - core), axis, 1).astype(F32)).astype(BF)
    if later is not None:
        later, both = lax.optimization_barrier((later, both))
    pick = lambda i: lax.dynamic_index_in_dim(both, i // 2, 0, keepdims=False)
    total = pick(me).astype(F32)
    for k in range(2, n, 2):
        total = total + swap(pick(me ^ k), axis, k).astype(F32)
    total = total.astype(BF)
    return total if later is None else (total, later)


def per_device(x_src, doc_lengths, doc_dests, w_gate, w_up, w_down, basis, dy):
    groups = doc_lengths.shape[0]
    tokens, recv = x_src.shape[0], dy.shape[0]
    width = w_gate.shape[1]
    high = lax.Precision.HIGH
    place = places(doc_lengths, doc_dests, tokens, recv)
    deal = (lax.broadcasted_iota(jnp.int32, (groups * recv, groups * tokens), 0) == place).astype(BF)

    x = gather(x_src, FS)
    dy, x = lax.optimization_barrier((dy, x))
    g = dot(x, w_gate).astype(BF)
    u = dot(x, w_up).astype(BF)
    q = dot(x.astype(F32), basis, precision=high).astype(BF)
    gate, up = scatter(g, DP), scatter(u, DP)
    sig = jax.nn.sigmoid(gate)
    hidden = (gate * sig * up).astype(BF)

    dy_all = dot(deal, gather(dy, FS, (g, u)), ROWS).astype(BF)
    both = scatter(jnp.concatenate([dot(dy_all, w_down, COLS).astype(BF), q], axis=1), DP)
    hg, keys = both[:, :width], both[:, width:]
    gate_grad = (hg * up * sig * (1.0 + gate * (1.0 - sig))).astype(BF)
    up_grad = (hg * gate * sig).astype(BF)

    hall = gather(hidden, DP)
    second = gather(jnp.concatenate([gate_grad, up_grad, keys.astype(BF)], axis=1), DP)
    ggall, ugall, kall = second[:, :width], second[:, width : 2 * width], second[:, 2 * width :]

    part = dot(hall, w_down).astype(BF)
    layer_out = scatter(dot(deal, part).astype(BF), FS)
    part = (dot(ggall, w_gate, COLS) + dot(ugall, w_up, COLS)).astype(BF)
    part = dot(deal, part).astype(BF)
    hall, part = lax.optimization_barrier((hall, part))
    x_proj = (x.astype(F32) - dot(kall.astype(F32), basis, COLS, precision=high)).astype(BF)
    input_grad, x_proj = scatter(part, FS, x_proj)
    grad_down = dot(hall, dy_all, ROWS)
    grad_gate = dot(x_proj, ggall, ROWS)
    grad_up = dot(x_proj, ugall, ROWS)
    return layer_out, input_grad, grad_gate, grad_up, grad_down


def solution(mesh):
    tiled = P(FS, DP)
    return jax.shard_map(
        per_device,
        mesh=mesh,
        in_specs=(tiled, P(), P(), P(DP, FS), P(DP, FS), tiled, P(DP, None), tiled),
        out_specs=(tiled, tiled, P(DP, FS), P(DP, FS), tiled),
        check_vma=False,
    )
```
